128 devices in a mesh: dp: 32 (over y, z, core), mp: 4 (over x).
Axes of the slice: x: 4, y: 4, z: 4, core: 2. Of those that a mesh axis runs over, the one named last changes fastest.
Arguments:
- frames: bfloat16 [32, 1024, 768], P('dp', 'mp'), may hold values from -6 to 6
- attend_gain: bfloat16 [768], P(('dp', 'mp')), may hold values from 0.5 to 1.5
- attend_shift: bfloat16 [768], P(('dp', 'mp')), may hold values from -3 to 3
- query_weight: bfloat16 [768, 768], P('dp', 'mp'), may hold values from -0.21875 to 0.21875
- query_bias: bfloat16 [768], P(('dp', 'mp')), may hold values from -3 to 3
- key_weight: bfloat16 [768, 768], P('dp', 'mp'), may hold values from -0.21875 to 0.21875
- value_weight: bfloat16 [768, 768], P('dp', 'mp'), may hold values from -0.21875 to 0.21875
- value_bias: bfloat16 [768], P(('dp', 'mp')), may hold values from -3 to 3
- out_weight: bfloat16 [768, 768], P('mp', 'dp'), may hold values from -3.5 to 3.5
- out_bias: bfloat16 [768], P(('dp', 'mp')), may hold values from -3 to 3
- feed_gain: bfloat16 [768], P(('dp', 'mp')), may hold values from 0.5 to 1.5
- feed_shift: bfloat16 [768], P(('dp', 'mp')), may hold values from -3 to 3
- inner_weight: bfloat16 [768, 3072], P('dp', 'mp'), may hold values from -0.21875 to 0.21875
- inner_bias: bfloat16 [3072], P(('dp', 'mp')), may hold values from -3 to 3
- outer_weight: bfloat16 [3072, 768], P('mp', 'dp'), may hold values from -0.109375 to 0.109375
- outer_bias: bfloat16 [768], P(('dp', 'mp')), may hold values from -3 to 3
- cotangent: bfloat16 [32, 1024, 768], P('dp', 'mp'), may hold values from -6 to 6
Outputs:
- output: bfloat16 [32, 1024, 768], P('dp', 'mp')
- frames_grad: bfloat16 [32, 1024, 768], P('dp', 'mp')
- attend_gain_grad: float32 [768], P(('dp', 'mp'))
- attend_shift_grad: float32 [768], P(('dp', 'mp'))
- query_weight_grad: float32 [768, 768], P('dp', 'mp')
- query_bias_grad: float32 [768], P(('dp', 'mp'))
- key_weight_grad: float32 [768, 768], P('dp', 'mp')
- value_weight_grad: float32 [768, 768], P('dp', 'mp')
- value_bias_grad: float32 [768], P(('dp', 'mp'))
- out_weight_grad: float32 [768, 768], P('mp', 'dp')
- out_bias_grad: float32 [768], P(('dp', 'mp'))
- feed_gain_grad: float32 [768], P(('dp', 'mp'))
- feed_shift_grad: float32 [768], P(('dp', 'mp'))
- inner_weight_grad: float32 [768, 3072], P('dp', 'mp')
- inner_bias_grad: float32 [3072], P(('dp', 'mp'))
- outer_weight_grad: float32 [3072, 768], P('mp', 'dp')
- outer_bias_grad: float32 [768], P(('dp', 'mp'))
The draws below stay inside these ranges and needn't reach their ends.
All inputs are finite; a program needn't handle non-finite values.
Results may differ from the reference program's by a relative error of at most 0.03.
Values may be sent and summed in bfloat16 or wider, within the bound.
No kernel may reach another device: no remote copies, remote signals or barrier semaphores. Data moves between devices by JAX's collectives and lax.ppermute only.
A program may use at most 64 MiB of HBM per device.

```python
import jax
import jax.numpy as jnp
from jax import lax

D = 768
H = 12
HD = 64
FF = 3072
FRAMES = 1024
CLIPS = 32


def strengthened(values, stream_key, source, target, blocks, factor):
    owner, partner = [(jnp.arange(values.shape[position]) // (values.shape[position] // blocks)).reshape([-1 if axis == position else 1 for axis in range(values.ndim)]) for position in (source, target)]
    chosen = jax.random.permutation(stream_key, blocks)[partner]
    strong = (owner == chosen) | (owner == (partner + blocks // 2) % blocks)
    return jnp.where(strong, factor * values, values)


def steps_of(own_key, dims, split, smallest, top_value):
    def one(dim, blocks):
        heights = jax.random.uniform(jax.random.fold_in(jax.random.fold_in(own_key, 6), dim), (blocks,), jnp.float32, smallest / len(split), top_value / len(split))
        return jnp.repeat(jnp.exp(heights), dims[dim] // blocks).reshape((-1,) + (1,) * (len(dims) - dim - 1))

    level = one(*split[0])
    for cut in split[1:]:
        level = level * one(*cut)
    return level


def noise(own_key, extent, width, bound, pieces=(), dtype=jnp.bfloat16):
    values = jax.random.normal(own_key, extent, jnp.float32) * width
    if len(pieces) > 0:
        values = steps_of(own_key, extent, pieces, -0.22, 0.18) * values
    return jnp.clip(values, min=-bound, max=bound).astype(dtype)


def bell_draw_with(key, dims, scale, limit, split, heavy, kind=jnp.bfloat16):
    values = scale * jax.random.normal(key, dims, jnp.float32)
    if split:
        values = values * steps_of(key, dims, split, -0.22, 0.18)
    return jnp.clip(strengthened(values, jax.random.fold_in(key, 3), *heavy), -limit, limit).astype(kind)


def setup_inputs(seed: int = 0) -> dict:
    seeds = jax.random.split(jax.random.key(seed), 18)
    frames = noise(seeds[0], (CLIPS, FRAMES, D), 1.0, 6.0, ((0, 32), (1, 4)))
    attend_gain = jnp.clip(1.0 + 0.1 * jax.random.normal(seeds[1], (D,), jnp.float32), 0.5, 1.5).astype(jnp.bfloat16)
    attend_shift = noise(seeds[2], (D,), 0.5, 3.0, ((0, 128),))
    query_weight = noise(seeds[3], (D, D), D ** -0.5, 0.21875, ((0, 32), (1, 4)))
    query_bias = noise(seeds[4], (D,), 0.5, 3.0, ((0, 128),))
    key_weight = noise(seeds[5], (D, D), D ** -0.5, 0.21875, ((0, 32), (1, 4)))
    value_weight = noise(seeds[6], (D, D), D ** -0.5, 0.21875, ((0, 32), (1, 4)))
    value_bias = noise(seeds[7], (D,), 0.5, 3.0, ((0, 128),))
    out_weight = noise(seeds[8], (D, D), (max(D // 256, 1)) ** -0.5, 3.5, ((0, 4), (1, 32)))
    out_bias = noise(seeds[9], (D,), 0.5, 3.0, ((0, 128),))
    feed_gain = jnp.clip(1.0 + 0.1 * jax.random.normal(seeds[10], (D,), jnp.float32), 0.5, 1.5).astype(jnp.bfloat16)
    feed_shift = noise(seeds[11], (D,), 0.5, 3.0, ((0, 128),))
    inner_weight = noise(seeds[12], (D, FF), D ** -0.5, 0.21875, ((0, 32), (1, 4)))
    inner_bias = noise(seeds[13], (FF,), 0.5, 3.0, ((0, 128),))
    outer_weight = noise(seeds[14], (FF, D), FF ** -0.5, 0.109375, ((0, 4), (1, 32)))
    outer_bias = noise(seeds[15], (D,), 0.5, 3.0, ((0, 128),))
    cotangent = bell_draw_with(seeds[16], (CLIPS, FRAMES, D), 1.0, 6.0, ((0, 32), (1, 4)), (0, 2, 32, 2.75))
    return dict(frames=frames, attend_gain=attend_gain, attend_shift=attend_shift, query_weight=query_weight, query_bias=query_bias, key_weight=key_weight, value_weight=value_weight, value_bias=value_bias, out_weight=out_weight, out_bias=out_bias, feed_gain=feed_gain, feed_shift=feed_shift, inner_weight=inner_weight, inner_bias=inner_bias, outer_weight=outer_weight, outer_bias=outer_bias, cotangent=cotangent)


@jax.custom_vjp
def low(v):
    return lax.optimization_barrier(v.astype(jnp.bfloat16)).astype(jnp.float32)

@jax.custom_vjp
def low_back(v):
    return v

def low_keep(v):
    return (low(v), None)

def low_pass(kept, grad):
    return (grad,)

def back_keep(v):
    return (v, None)

def back_low(kept, grad):
    return (low(grad),)
low.defvjp(low_keep, low_pass)
low_back.defvjp(back_keep, back_low)

def matmul(left, right):
    return jnp.dot(left, right, precision=lax.Precision.HIGHEST)

def layer_norm(rows, gain, shift):
    centred = rows - lax.optimization_barrier(jnp.mean(rows, axis=-1, keepdims=True))
    variance = lax.optimization_barrier(jnp.mean(centred * centred, axis=-1, keepdims=True))
    return centred * lax.rsqrt(variance + 1e-05) * gain + shift

def attend(parts):
    query, keys, values = parts
    scores = low_back(jnp.einsum('qhd,khd->hqk', query, keys, precision=lax.Precision.HIGHEST) * HD ** (-0.5))
    probs = jax.nn.softmax(scores, axis=-1)
    return jnp.einsum('hqk,khd->qhd', low(probs), values, precision=lax.Precision.HIGHEST)

def forward(source, attend_gain, attend_shift, query_weight, query_bias, key_weight, value_weight, value_bias, out_weight, out_bias, feed_gain, feed_shift, inner_weight, inner_bias, outer_weight, outer_bias):
    normed_one = low(layer_norm(source, attend_gain, attend_shift))
    queries = low(low_back(matmul(normed_one, query_weight)) + query_bias)
    keys = low(low_back(matmul(normed_one, key_weight)))
    values = low(low_back(matmul(normed_one, value_weight)) + value_bias)
    shape = source.shape[:2] + (H, HD)
    mixed = lax.map(jax.checkpoint(attend), (queries.reshape(shape), keys.reshape(shape), values.reshape(shape)))
    mixed = low_back(low(mixed.reshape(source.shape)))
    middle = source + low_back(matmul(mixed, out_weight)) + out_bias
    normed_two = low(layer_norm(middle, feed_gain, feed_shift))
    inner = low_back(matmul(normed_two, inner_weight)) + inner_bias
    active = low(jax.nn.gelu(inner, approximate=False))
    return middle + low_back(matmul(active, outer_weight)) + outer_bias

def reference(frames, attend_gain, attend_shift, query_weight, query_bias, key_weight, value_weight, value_bias, out_weight, out_bias, feed_gain, feed_shift, inner_weight, inner_bias, outer_weight, outer_bias, cotangent):
    inputs = [a.astype(jnp.float32) for a in (frames, attend_gain, attend_shift, query_weight, query_bias, key_weight, value_weight, value_bias, out_weight, out_bias, feed_gain, feed_shift, inner_weight, inner_bias, outer_weight, outer_bias)]
    result, pullback = jax.vjp(forward, *inputs)
    grads = pullback(cotangent.astype(jnp.float32))
    return (result.astype(jnp.bfloat16), grads[0].astype(jnp.bfloat16), grads[1], grads[2], grads[3], grads[4], grads[5], grads[6], grads[7], grads[8], grads[9], grads[10], grads[11], grads[12], grads[13], grads[14], grads[15])
```

```python
from functools import partial

import jax
import jax.numpy as jnp
from jax import lax
from jax.sharding import PartitionSpec as P

HD = 64
MP = 4
SIDE = 4
CORES = 2
EPS = 1e-05

F32 = jnp.float32
BF16 = jnp.bfloat16


def product(left, right):
    return jnp.dot(left, right, preferred_element_type=F32)


def contract(spec, left, right):
    return jnp.einsum(spec, left, right, preferred_element_type=F32)


def normalize(rows, gain, shift):
    centred = rows - jnp.mean(rows, axis=-1, keepdims=True)
    inverse = lax.rsqrt(jnp.mean(centred * centred, axis=-1, keepdims=True) + EPS)
    scaled = centred * inverse
    return (scaled * gain + shift, scaled, inverse)


def normalize_back(grad, scaled, inverse, gain):
    weighted = grad * gain
    rows_grad = inverse * (
        weighted
        - jnp.mean(weighted, axis=-1, keepdims=True)
        - scaled * jnp.mean(weighted * scaled, axis=-1, keepdims=True)
    )
    return (rows_grad, jnp.sum(grad * scaled, axis=0), jnp.sum(grad, axis=0))


def shift_mp(piece, step):
    return lax.ppermute(piece, "mp", [(i, (i + step) % MP) for i in range(MP)])


def spread_rows(rows):
    return [rows] + [shift_mp(rows, k) for k in range(1, MP)]


def collect_rows(parts):
    total = parts[0].astype(F32)
    for k in range(1, MP):
        total = total + shift_mp(parts[k].astype(BF16), MP - k).astype(F32)
    return total


def dp_moves(step_y, step_z, step_c):
    pairs = []
    for y in range(SIDE):
        for z in range(SIDE):
            for c in range(CORES):
                target = ((y + step_y) % SIDE, (z + step_z) % SIDE, (c + step_c) % CORES)
                pairs.append(
                    ((y * SIDE + z) * CORES + c, (target[0] * SIDE + target[1]) * CORES + target[2])
                )
    return pairs


def shift_dp(piece, step_y, step_z, step_c):
    return lax.ppermute(piece, "dp", dp_moves(step_y, step_z, step_c))


def turned(stack, offset):
    return lax.dynamic_slice_in_dim(
        jnp.concatenate([stack, stack], axis=0), offset, stack.shape[0], axis=0
    )


def gather_dp(piece, place):
    y, z, c = place
    found = jnp.stack([piece] + [shift_dp(piece, 0, SIDE - k, 0) for k in range(1, SIDE)])
    found = turned(found, (SIDE - z) % SIDE)
    found = jnp.stack([found] + [shift_dp(found, SIDE - k, 0, 0) for k in range(1, SIDE)])
    found = turned(found, (SIDE - y) % SIDE)
    other = shift_dp(found, 0, 0, 1)
    first = jnp.where(c == 0, found, other)
    second = jnp.where(c == 0, other, found)
    return jnp.stack([first, second], axis=2)


def reduce_dp(blocks, place):
    y, z, c = place
    other = lax.dynamic_index_in_dim(blocks, 1 - c, axis=2, keepdims=False).astype(BF16)
    mine = lax.dynamic_index_in_dim(blocks, c, axis=2, keepdims=False).astype(F32)
    total = mine + shift_dp(other, 0, 0, 1).astype(F32)
    total = turned(total.astype(BF16), y)
    total = total[0].astype(F32) + sum(
        shift_dp(total[k], k, 0, 0).astype(F32) for k in range(1, SIDE)
    )
    total = turned(total.astype(BF16), z)
    return total[0].astype(F32) + sum(
        shift_dp(total[k], 0, k, 0).astype(F32) for k in range(1, SIDE)
    )


def attend_block(query_block, keys, values, factor):
    scores = contract("qhd,khd->hqk", query_block, keys) * factor
    highest = jnp.max(scores, axis=-1, keepdims=True)
    expd = jnp.exp(scores - highest)
    totals = jnp.sum(expd, axis=-1, keepdims=True)
    probs = expd / totals
    mixed = contract("hqk,khd->qhd", probs.astype(BF16), values)
    return (mixed, (highest + jnp.log(totals))[..., 0])


def attend_back(keys, values, factor, carry, block):
    key_total, value_total = carry
    query_block, log_total, grad_block = block
    scores = contract("qhd,khd->hqk", query_block, keys) * factor
    probs = jnp.exp(scores - log_total[..., None])
    prob_grad = contract("qhd,khd->hqk", grad_block, values)
    score_grad = (
        probs * (prob_grad - jnp.sum(probs * prob_grad, axis=-1, keepdims=True))
    ).astype(BF16)
    value_total = value_total + contract("hqk,qhd->khd", probs.astype(BF16), grad_block)
    key_total = key_total + contract("hqk,qhd->khd", score_grad, query_block) * factor
    query_grad = contract("hqk,khd->qhd", score_grad, keys) * factor
    return ((key_total, value_total), query_grad)


def place_piece(piece, total, position):
    return lax.dynamic_update_slice_in_dim(
        jnp.zeros((total,), F32), piece, position * piece.shape[0], 0
    )


def shards(
    frames,
    attend_gain,
    attend_shift,
    query_weight,
    query_bias,
    key_weight,
    value_weight,
    value_bias,
    out_weight,
    out_bias,
    feed_gain,
    feed_shift,
    inner_weight,
    inner_bias,
    outer_weight,
    outer_bias,
    cotangent,
):
    position = lax.axis_index("mp")
    column = lax.axis_index("dp")
    place = (column // (SIDE * CORES), (column // CORES) % SIDE, column % CORES)
    devices = SIDE * SIDE * CORES * MP
    rows = frames.shape[1]
    model = frames.shape[2]
    width = query_weight.shape[1]
    hidden = inner_weight.shape[1]
    depth = query_weight.shape[0]
    heads = width // HD
    factor = HD ** (-0.5)

    raw = spread_rows(frames[0])
    qkv = gather_dp(jnp.concatenate([query_weight, key_weight, value_weight], axis=1), place)
    qkv = qkv.reshape(model, 3 * width)
    rest = lax.all_gather(
        jnp.concatenate([inner_weight, outer_weight.T, out_weight.T], axis=1),
        "dp",
        axis=0,
        tiled=True,
    )
    inner_all = rest[:, :hidden]
    outer_all = rest[:, hidden : 2 * hidden]
    out_all = rest[:, 2 * hidden :]
    vectors = (
        attend_gain,
        attend_shift,
        query_bias,
        value_bias,
        out_bias,
        feed_gain,
        feed_shift,
        outer_bias,
        inner_bias,
    )
    packed = jnp.concatenate(vectors)
    packed = lax.all_to_all(
        jnp.broadcast_to(packed[None], (devices,) + packed.shape),
        ("dp", "mp"),
        0,
        0,
        tiled=True,
    )
    each = attend_gain.shape[0]
    small = packed[:, : 8 * each].reshape(devices, 8, each).transpose(1, 0, 2).reshape(8, model)
    small = small.astype(F32)
    inner_bias_all = packed[:, 8 * each :].reshape(MP * hidden).astype(F32)
    first_gain, first_shift, query_all, value_all = small[0], small[1], small[2], small[3]
    output_offset, second_gain, second_shift, outer_offset = small[4], small[5], small[6], small[7]
    query_offset = lax.dynamic_slice_in_dim(query_all, position * width, width)
    value_offset = lax.dynamic_slice_in_dim(value_all, position * width, width)
    inner_offset = lax.dynamic_slice_in_dim(inner_bias_all, position * hidden, hidden)
    upstream_low = cotangent[0]
    full_up = jnp.concatenate(spread_rows(upstream_low))

    source = frames[0].astype(F32)
    _, scaled_one, inverse_one = normalize(source, first_gain, first_shift)
    full_raw = jnp.concatenate(raw).astype(F32)
    full_one = normalize(full_raw, first_gain, first_shift)[0].astype(BF16)
    length = full_one.shape[0]
    block = min(512, length)
    count = length // block
    offset = jnp.concatenate([query_offset, jnp.zeros_like(query_offset), value_offset])
    triple = (product(full_one, qkv) + offset).astype(BF16)
    queries, keys, values = (triple[:, i * width : (i + 1) * width] for i in range(3))
    key_heads = keys.reshape(length, heads, HD)
    value_heads = values.reshape(length, heads, HD)
    query_blocks = queries.reshape(count, block, heads, HD)
    mixed, log_totals = lax.map(
        partial(attend_block, keys=key_heads, values=value_heads, factor=factor), query_blocks
    )
    mixed_low = mixed.reshape(length, width).astype(BF16)

    def parts(whole):
        return [whole[k * rows : (k + 1) * rows] for k in range(MP)]

    attended = collect_rows([contract("tc,dc->td", part, out_all) for part in parts(mixed_low)])
    middle = source + attended + output_offset
    normed_two, scaled_two, inverse_two = normalize(middle, second_gain, second_shift)
    full_two = jnp.concatenate(spread_rows(normed_two.astype(BF16)))
    inner = product(full_two, inner_all) + inner_offset
    active, gelu_pull = jax.vjp(partial(jax.nn.gelu, approximate=False), inner)
    active = active.astype(BF16)
    active_grad = product(full_up, outer_all)
    inner_grad = gelu_pull(active_grad)[0]
    inner_low = inner_grad.astype(BF16)
    second_rows = collect_rows(
        [contract("tf,df->td", part, inner_all) for part in parts(inner_low)]
    )
    middle_norm_grad, second_gain_grad, second_shift_grad = normalize_back(
        second_rows, scaled_two, inverse_two, second_gain
    )
    upstream = upstream_low.astype(F32)
    middle_grad = upstream + middle_norm_grad
    full_middle = jnp.concatenate(spread_rows(middle_grad.astype(BF16)))

    fed = collect_rows([contract("tf,df->td", part, outer_all) for part in parts(active)])
    output = (middle + fed + outer_offset).astype(BF16)[None]
    feed_grads = jnp.concatenate(
        [
            contract("td,tf->df", full_two, inner_low).astype(BF16),
            contract("td,tf->df", full_up, active).astype(BF16),
        ],
        axis=1,
    )
    feed_sums = lax.psum_scatter(feed_grads, "dp", scatter_dimension=0, tiled=True).astype(F32)

    mixed_grad = product(full_middle, out_all).astype(BF16)
    grad_blocks = mixed_grad.reshape(count, block, heads, HD)
    zeros = jnp.zeros((length, heads, HD), F32)
    (key_total, value_total), query_parts = lax.scan(
        partial(attend_back, key_heads, value_heads, factor),
        (zeros, zeros),
        (query_blocks, log_totals, grad_blocks),
    )
    query_grad = query_parts.reshape(length, width)
    key_grad = key_total.reshape(length, width)
    value_grad = value_total.reshape(length, width)
    triple_low = jnp.concatenate(
        [query_grad.astype(BF16), key_grad.astype(BF16), value_grad.astype(BF16)], axis=1
    )
    first_rows = collect_rows([contract("tc,dc->td", part, qkv) for part in parts(triple_low)])
    attend_grads = jnp.concatenate(
        [
            contract("td,tc->dc", full_one, triple_low).astype(BF16),
            contract("td,tc->dc", full_middle, mixed_low).astype(BF16),
        ],
        axis=1,
    )
    attend_sums = reduce_dp(
        attend_grads.reshape(SIDE, SIDE, CORES, depth, 4 * width), place
    )
    source_norm_grad, first_gain_grad, first_shift_grad = normalize_back(
        first_rows, scaled_one, inverse_one, first_gain
    )
    frames_grad = (middle_grad + source_norm_grad).astype(BF16)[None]
    sums = jnp.stack(
        [
            first_gain_grad,
            first_shift_grad,
            place_piece(jnp.sum(query_grad, axis=0), model, position),
            place_piece(jnp.sum(value_grad, axis=0), model, position),
            jnp.sum(middle_grad, axis=0),
            second_gain_grad,
            second_shift_grad,
            jnp.sum(upstream, axis=0),
        ]
    )
    sums = sums.reshape(8, devices, each).transpose(1, 0, 2).reshape(devices, 8 * each)
    inner_sums = place_piece(jnp.sum(inner_grad, axis=0), MP * hidden, position)
    sums = jnp.concatenate([sums, inner_sums.reshape(devices, MP * each)], axis=1)
    sums = jnp.sum(lax.all_to_all(sums, ("dp", "mp"), 0, 0, tiled=True), axis=0)
    pieces = [sums[i * each : (i + 1) * each] for i in range(8)]
    return (
        output,
        frames_grad,
        pieces[0],
        pieces[1],
        attend_sums[:, :width],
        pieces[2],
        attend_sums[:, width : 2 * width],
        attend_sums[:, 2 * width : 3 * width],
        pieces[3],
        attend_sums[:, 3 * width :].T,
        pieces[4],
        pieces[5],
        pieces[6],
        feed_sums[:, :hidden],
        sums[8 * each :],
        feed_sums[:, hidden:].T,
        pieces[7],
    )


def solution(mesh):
    rows = P("dp", "mp", None)
    vector = P(("dp", "mp"))
    wide = P("dp", "mp")
    tall = P("mp", "dp")
    in_specs = (
        rows, vector, vector, wide, vector, wide, wide, vector, tall, vector,
        vector, vector, wide, vector, tall, vector, rows,
    )
    out_specs = (
        rows, rows, vector, vector, wide, vector, wide, wide, vector, tall,
        vector, vector, vector, wide, vector, tall, vector,
    )
    return jax.shard_map(shards, mesh=mesh, in_specs=in_specs, out_specs=out_specs, check_vma=False)
```

```python
from functools import partial

import jax
import jax.numpy as jnp
import numpy as np
from jax import lax
from jax.experimental import pallas as pl
from jax.experimental.pallas import tpu as pltpu
from jax.sharding import Mesh
from jax.sharding import PartitionSpec as P

HD = 64
MP = 4
PLANE = 16
CORES = 2
EPS = 1e-05

F32 = jnp.float32
BF16 = jnp.bfloat16


def shift_mp(piece, step):
    return lax.ppermute(piece, "mp", [(i, (i + step) % MP) for i in range(MP)])


def spread_rows(rows):
    return [rows] + [shift_mp(rows, k) for k in range(1, MP)]


def swap_cores(piece):
    return lax.ppermute(piece, "core", [(0, 1), (1, 0)])


def exchange_plane(blocks):
    return lax.all_to_all(blocks, "yz", 0, 0, tiled=True)


def join_cores(found, other, core):
    both = jnp.stack(
        [jnp.where(core == 0, found, other), jnp.where(core == 0, other, found)], axis=1
    )
    return both.reshape(2 * found.shape[0] * found.shape[1], found.shape[2])


def turn_over(matrix):
    unit = jnp.eye(matrix.shape[1], dtype=BF16)
    return lax.dot_general(unit, matrix, (((1,), (1,)), ((), ())), preferred_element_type=F32)


def gelu_parts(inner):
    density = jnp.exp(-0.5 * inner * inner)
    size = jnp.abs(inner) * (0.5**0.5)
    t = 1.0 / (1.0 + 0.3275911 * size)
    poly = 1.061405429
    for term in (-1.453152027, 1.421413741, -0.284496736, 0.254829592):
        poly = poly * t + term
    tail = 0.5 * poly * t * density
    return (jnp.where(inner < 0, tail, 1.0 - tail), density * 0.3989422804014327)


def vmem_call(kernel, outs, flops, *operands, scratch=(), limit=20):
    size = sum(a.size * a.dtype.itemsize for a in operands) + sum(
        o.size * o.dtype.itemsize for o in outs
    )
    return pl.pallas_call(
        kernel,
        out_shape=tuple(outs),
        in_specs=[
            pl.BlockSpec(memory_space=pltpu.SMEM if a.dtype == jnp.int32 else pltpu.VMEM)
            for a in operands
        ],
        out_specs=tuple(pl.BlockSpec(memory_space=pltpu.VMEM) for _ in outs),
        scratch_shapes=list(scratch),
        compiler_params=pltpu.CompilerParams(vmem_limit_bytes=limit * 2**20),
        cost_estimate=pl.CostEstimate(flops=flops, bytes_accessed=size, transcendentals=0),
    )(*operands)


def array(shape, dtype=BF16):
    return jax.ShapeDtypeStruct(shape, dtype)


def dot(left, right, sides=(1, 0)):
    return lax.dot_general(
        left, right, (((sides[0],), (sides[1],)), ((), ())), preferred_element_type=F32
    )


def scaled_rows(rows):
    centred = rows - jnp.mean(rows, axis=-1, keepdims=True)
    inverse = lax.rsqrt(jnp.mean(centred * centred, axis=-1, keepdims=True) + EPS)
    return (centred * inverse, inverse)


def first_pack_kernel(c0, c1, c2, c3, query, key, value, out):
    width = query.shape[1]
    pieces = [c[:, :width] for c in (c0, c1, c2, c3)] + [query[...], key[...], value[...]]
    for i, piece in enumerate(pieces):
        for k in range(out.shape[0]):
            out[k, :, i * width : (i + 1) * width] = piece
    vectors = c0[:, width:].astype(F32)
    for c in (c1, c2, c3):
        vectors = vectors + c[:, width:].astype(F32)
    for k in range(out.shape[0]):
        out[k, :, len(pieces) * width :] = vectors.astype(BF16)


def feed_pack_kernel(inner, turned_outer, out):
    out[:, : inner.shape[1]] = inner[...]
    out[:, inner.shape[1] :] = turned_outer[...]


def slot_rows(position, k, rows):
    return pl.ds(pl.multiple_of(lax.rem(position[0] + MP - k, MP) * rows, rows), rows)


def attend_kernel(factor, position, raw, weight, norms, offset, normed, triple, turned_low, m0, m1, m2, m3, log_totals):
    rows, length = m0.shape[0], normed.shape[0]
    width = m0.shape[1]
    for k in range(MP):
        scaled, _ = scaled_rows(raw[slot_rows(position, k, rows), :].astype(F32))
        low = (scaled * norms[0:1, :] + norms[1:2, :]).astype(BF16)
        normed[k * rows : (k + 1) * rows, :] = low
        projected = dot(low, weight[:, 4 * width : 7 * width]) + offset[...]
        triple[k * rows : (k + 1) * rows, :] = projected.astype(BF16)
        turned_low[:, k * rows : (k + 1) * rows] = projected.T.astype(BF16)
    for h in range(width // HD):
        keys = triple[:, width + h * HD : width + (h + 1) * HD]
        values = turned_low[2 * width + h * HD : 2 * width + (h + 1) * HD, :]
        for k, mixed in enumerate((m0, m1, m2, m3)):
            block = slice(k * rows, (k + 1) * rows)
            queries = turned_low[h * HD : (h + 1) * HD, block] * factor
            scores = dot(keys, queries)
            highest = jnp.max(scores, axis=0, keepdims=True)
            expd = jnp.exp(scores - highest)
            totals = jnp.sum(expd, axis=0, keepdims=True)
            found = dot(values, expd.astype(BF16)) / totals
            mixed[:, h * HD : (h + 1) * HD] = found.T.astype(BF16)
            log_totals[h : h + 1, block] = highest + jnp.log(totals)


def attend_back_kernel(
    factor, triple, turned_low, log_totals, g0, g1, g2, g3, weight,
    triple_low, p0, p1, p2, p3, sums, total,
):
    rows, width = g0.shape
    total[...] = jnp.zeros_like(total)
    turned_grads = [g[...].astype(F32).T.astype(BF16) for g in (g0, g1, g2, g3)]
    for h in range(width // HD):
        head = slice(h * HD, (h + 1) * HD)
        keys = triple[:, width + h * HD : width + (h + 1) * HD]
        values = triple[:, 2 * width + h * HD : 2 * width + (h + 1) * HD]
        turned_keys = turned_low[width + h * HD : width + (h + 1) * HD, :]
        key_grad, value_grad = 0.0, 0.0
        for k, g in enumerate((g0, g1, g2, g3)):
            block = slice(k * rows, (k + 1) * rows)
            scores = dot(keys, turned_low[head, block] * factor)
            probs = jnp.exp(scores - log_totals[h : h + 1, block])
            prob_grad = dot(values, turned_grads[k][head, :])
            inside = jnp.sum(probs * prob_grad, axis=0, keepdims=True)
            score_grad = (probs * (prob_grad - inside)).astype(BF16)
            value_grad = value_grad + dot(probs.astype(BF16), g[:, head])
            key_grad = key_grad + dot(score_grad, triple[block, head])
            total[block, head] = (dot(turned_keys, score_grad) * float(factor)).T
        total[:, width + h * HD : width + (h + 1) * HD] = key_grad * float(factor)
        total[:, 2 * width + h * HD : 2 * width + (h + 1) * HD] = value_grad
    sums[...] = jnp.sum(total[...], axis=0, keepdims=True)
    for k, out in enumerate((p0, p1, p2, p3)):
        block = slice(k * rows, (k + 1) * rows)
        low = total[block, :].astype(BF16)
        triple_low[block, :] = low
        out[...] = dot(low, weight[:, 4 * width : 7 * width], (1, 1)).astype(BF16)


def middle_kernel(m0, m1, m2, m3, weight, source, norms, middle, normed):
    total = source[...].astype(F32) + norms[2:3, :]
    width = m0.shape[1]
    for k, m in enumerate((m0, m1, m2, m3)):
        total = total + dot(m[...], weight[:, k * width : (k + 1) * width], (1, 1))
    middle[...] = total
    scaled, _ = scaled_rows(total)
    normed[...] = (scaled * norms[0:1, :] + norms[1:2, :]).astype(BF16)


def feed_kernel(k, last, position, core, normed, up, weights, offset, *refs):
    if k > 0:
        grads_in, fed_in, sums_in, *refs = refs
    if last:
        second, mine, other, fed, sums, grads = refs
    else:
        second, grads, fed, sums = refs
    rows = normed.shape[0]
    hidden = weights.shape[1] // 2
    inner = dot(normed[...], weights[:, :hidden]) + offset[...]
    whole, density = gelu_parts(inner)
    active = (inner * whole).astype(BF16)
    grad = dot(up[...], weights[:, hidden:]) * (whole + inner * density)
    low = grad.astype(BF16)
    second[...] = dot(low, weights[:, :hidden], (1, 1)).astype(BF16)
    sum_here = jnp.sum(grad, axis=0, keepdims=True)
    turned_normed = normed[...].astype(F32).T.astype(BF16)
    turned_up = up[...].astype(F32).T.astype(BF16)
    if k > 0:
        fed[...] = fed_in[...]
        sums[...] = sums_in[...] + sum_here
        grads[:, :hidden] = grads_in[:, :hidden] + dot(turned_normed, low)
        grads[:, hidden:] = grads_in[:, hidden:] + dot(turned_up, active)
    else:
        sums[...] = sum_here
        grads[:, :hidden] = dot(turned_normed, low)
        grads[:, hidden:] = dot(turned_up, active)
    fed[slot_rows(position, k, rows), :] = dot(active, weights[:, hidden:], (1, 1)).astype(BF16)
    if last:
        depth = mine.shape[1]
        for i in range(mine.shape[0]):
            start = pl.multiple_of((2 * i + core[0]) * depth, 8)
            mine[i] = grads[pl.ds(start, depth), :].astype(BF16)
            start = pl.multiple_of((2 * i + 1 - core[0]) * depth, 8)
            other[i] = grads[pl.ds(start, depth), :].astype(BF16)


def middle_back_kernel(
    s0, s1, s2, s3, middle, up, norms, weight, m0, m1, m2, m3,
    middle_grad, h0, h1, h2, h3, o0, o1, o2, o3, sums,
):
    grad = s0[...].astype(F32)
    for s in (s1, s2, s3):
        grad = grad + s[...].astype(F32)
    scaled, inverse = scaled_rows(middle[...])
    weighted = grad * norms[0:1, :]
    upstream = up[...].astype(F32)
    total = upstream + inverse * (
        weighted
        - jnp.mean(weighted, axis=-1, keepdims=True)
        - scaled * jnp.mean(weighted * scaled, axis=-1, keepdims=True)
    )
    middle_grad[...] = total
    low = total.astype(BF16)
    turned = total.T.astype(BF16)
    for m, o in ((m0, o0), (m1, o1), (m2, o2), (m3, o3)):
        o[...] = dot(turned, m[...]).astype(BF16)
    width = h0.shape[1]
    for k, h in enumerate((h0, h1, h2, h3)):
        h[...] = dot(low, weight[:, k * width : (k + 1) * width]).astype(BF16)
    sums[0:1, :] = jnp.sum(total, axis=0, keepdims=True)
    sums[1:2, :] = jnp.sum(grad * scaled, axis=0, keepdims=True)
    sums[2:3, :] = jnp.sum(grad, axis=0, keepdims=True)
    sums[3:4, :] = jnp.sum(upstream, axis=0, keepdims=True)


def rows_back_kernel(p0, p1, p2, p3, source, gain, middle_grad, out):
    grad = p0[...].astype(F32)
    for p in (p1, p2, p3):
        grad = grad + p[...].astype(F32)
    scaled, inverse = scaled_rows(source[...].astype(F32))
    weighted = grad * gain[...]
    back = inverse * (
        weighted
        - jnp.mean(weighted, axis=-1, keepdims=True)
        - scaled * jnp.mean(weighted * scaled, axis=-1, keepdims=True)
    )
    out[...] = (middle_grad[...] + back).astype(BF16)


def last_grad_kernel(
    core, position, normed, triple_low, weight, o0, o1, o2, o3, norms, middle_sums, local_sums,
    mine, other, total,
):
    depth = mine.shape[1]
    third = triple_low.shape[1]
    width = third // 3
    model = weight.shape[0]
    grads = dot(normed[...].astype(F32).T.astype(BF16), triple_low[...])
    total[:, :third] = grads
    out_grad = o0[...].astype(F32)
    for o in (o1, o2, o3):
        out_grad = out_grad + o[...].astype(F32)
    total[:, third : third + width] = out_grad
    wide = weight[:, weight.shape[0] : weight.shape[0] + third].astype(F32)
    row_sum = jnp.sum(triple_low[...].astype(F32), axis=0, keepdims=True)
    shift_grad = jnp.sum(wide * row_sum, axis=1, keepdims=True)
    gain_grad = jnp.sum(wide * grads, axis=1, keepdims=True)
    turned_norms = norms[...].T
    gain_grad = (gain_grad - turned_norms[:, 1:2] * shift_grad) / turned_norms[:, 0:1]
    start = third + width
    total[:, start:] = jnp.zeros((model, total.shape[1] - start), F32)
    total[:, start : start + 1] = gain_grad
    total[:, start + 1 : start + 2] = shift_grad
    total[:, start + 2 : start + 6] = middle_sums[...].T
    row = pl.multiple_of(position[0] * width, 8)
    total[pl.ds(row, width), start + 6 : start + 12] = local_sums[...].T
    for i in range(mine.shape[0]):
        first = pl.multiple_of((2 * i + core[0]) * depth, 8)
        mine[i] = total[pl.ds(first, depth), :].astype(BF16)
        first = pl.multiple_of((2 * i + 1 - core[0]) * depth, 8)
        other[i] = total[pl.ds(first, depth), :].astype(BF16)


def shards(
    frames,
    attend_gain,
    attend_shift,
    query_weight,
    query_bias,
    key_weight,
    value_weight,
    value_bias,
    out_weight,
    out_bias,
    feed_gain,
    feed_shift,
    inner_weight,
    inner_bias,
    outer_weight,
    outer_bias,
    cotangent,
):
    position = lax.axis_index("mp")
    core = lax.axis_index("core")
    rows = frames.shape[1]
    length = rows * MP
    model = frames.shape[2]
    width = query_weight.shape[1]
    hidden = inner_weight.shape[1]
    depth = query_weight.shape[0]
    each = attend_gain.shape[0]
    heads = width // HD
    factor = HD ** (-0.5)
    slots = range(MP)
    core_index = core.reshape(1)
    position_index = position.reshape(1)

    vectors = 8 + MP
    pieces = (
        attend_gain,
        attend_shift,
        query_bias,
        value_bias,
        out_bias,
        feed_gain,
        feed_shift,
        outer_bias,
        inner_bias,
    )
    packed = sum(
        jnp.pad(v.astype(F32), (i * each, (8 + MP) * each - i * each - v.shape[0]))
        for i, v in enumerate(pieces)
    )
    entry = np.arange(vectors * each)
    early = entry < 8 * each
    row_of = np.where(early, entry % each, (entry - 8 * each) // MP)
    column_of = np.where(early, entry // each, 8 + (entry - 8 * each) % MP)
    to_column = jnp.asarray(column_of[:, None] == np.arange(vectors)[None], BF16)
    at_row = lax.iota(jnp.int32, depth)[:, None] == position * each + jnp.asarray(row_of, jnp.int32)
    piece = dot(jnp.where(at_row, packed[None], 0).astype(BF16), to_column).astype(BF16)
    carried = jnp.concatenate([turn_over(out_weight).astype(BF16), piece], axis=1)
    carried = [carried] + [shift_mp(carried, MP - k) for k in range(1, MP)]
    full_raw = lax.all_gather(frames[0], "mp", axis=0, tiled=True)
    (first_blocks,) = vmem_call(
        first_pack_kernel,
        [array((PLANE, depth, model + 3 * width + vectors))],
        10**6,
        *carried,
        query_weight,
        key_weight,
        value_weight,
        limit=4,
    )
    found = exchange_plane(first_blocks)
    inner_weight, outer_weight, found = lax.optimization_barrier(
        (inner_weight, outer_weight, found)
    )
    (feed_block,) = vmem_call(
        feed_pack_kernel, [array((depth, 2 * hidden))], 10**6, inner_weight, outer_weight.T, limit=4
    )
    feed_all = lax.all_gather(feed_block, ("yz", "core"), axis=0, tiled=True)
    first_all = join_cores(found, swap_cores(found), core)
    small = first_all[:, model + 3 * width :].T.astype(F32)
    first_norms = small[0:2]
    second_norms = jnp.stack([small[5], small[6], small[4]])
    local = lax.dynamic_slice_in_dim(small, position * width, width, axis=1)
    offset = jnp.concatenate([local[2], jnp.zeros_like(local[2]), local[3]])[None]
    inner_offset = local[8:].T.reshape(1, MP * width)

    rows_out = array((rows, model))
    heads_out = array((rows, width))
    normed, triple, turned_low, m0, m1, m2, m3, log_totals = vmem_call(
        partial(attend_kernel, factor),
        [
            array((length, model)),
            array((length, 3 * width)),
            array((3 * width, length)),
            heads_out,
            heads_out,
            heads_out,
            heads_out,
            array((heads, length), F32),
        ],
        4 * 10**9,
        position_index,
        full_raw,
        first_all,
        first_norms,
        offset,
        limit=18,
    )
    upstream_low = cotangent[0]
    ups = spread_rows(upstream_low)
    m1, m2, m3, *ups = lax.optimization_barrier((m1, m2, m3, *ups))
    own_mixed = [m0] + [shift_mp(m, MP - k) for k, m in ((1, m1), (2, m2), (3, m3))]
    middle, normed_two = vmem_call(
        middle_kernel,
        [array((rows, model), F32), rows_out],
        10**9,
        *own_mixed,
        first_all,
        frames[0],
        second_norms,
        limit=10,
    )
    twos = [normed_two, shift_mp(normed_two, 1), None, shift_mp(normed_two, MP - 1)]
    seconds, carry = {}, ()
    inner_sums = array((1, hidden), F32)
    feed_blocks = array((PLANE, depth, 2 * hidden))
    for k in (0, 1, 3, 2):
        last = k == 2
        grads = array((model, 2 * hidden), F32)
        fed_out = array((length, model))
        outs = [rows_out, feed_blocks, feed_blocks, fed_out, inner_sums]
        found = vmem_call(
            partial(feed_kernel, k, last),
            outs if last else [rows_out, grads, fed_out, inner_sums],
            5 * 10**9,
            position_index,
            core_index,
            twos[k],
            ups[k],
            feed_all,
            inner_offset,
            *carry,
            scratch=[pltpu.VMEM(grads.shape, F32)] if last else [],
            limit=16,
        )
        seconds[k] = found[0]
        if last:
            feed_mine, feed_other, fed_all, inner_total = found[1:]
        else:
            carry = found[1:]
        if k == 0:
            twos[1], twos[3], _ = lax.optimization_barrier((twos[1], twos[3], carry[2]))
            far = (shift_mp(twos[1][: rows // 2], 1), shift_mp(twos[3][rows // 2 :], MP - 1))
        if k == 3:
            *far, _ = lax.optimization_barrier((*far, carry[2]))
            twos[2] = jnp.concatenate(far)
    seconds = [seconds[0]] + [shift_mp(seconds[k], MP - k) for k in range(1, MP)]
    middle_grad, h0, h1, h2, h3, o0, o1, o2, o3, middle_sums = vmem_call(
        middle_back_kernel,
        [
            array((rows, model), F32),
            *[heads_out] * MP,
            *[array((model, width))] * MP,
            array((4, model), F32),
        ],
        10**9,
        *seconds,
        middle,
        upstream_low,
        second_norms,
        first_all,
        *own_mixed,
        limit=12,
    )
    mixed_grads = [h0] + [shift_mp(h, k) for k, h in ((1, h1), (2, h2), (3, h3))]
    out_grads = [o0] + [shift_mp(o, k) for k, o in ((1, o1), (2, o2), (3, o3))]
    fed_all, mixed_grads[0], mixed_grads[2] = lax.optimization_barrier(
        (fed_all, mixed_grads[0], mixed_grads[2])
    )
    fed = lax.psum_scatter(fed_all, "mp", scatter_dimension=0, tiled=True)
    output = middle + small[7] + fed.astype(F32)
    output = output.astype(BF16)[None]
    feed_mine, feed_other, h1 = lax.optimization_barrier((feed_mine, feed_other, h1))
    feed_total = feed_mine.astype(F32) + swap_cores(feed_other).astype(F32)
    feed_total = exchange_plane(feed_total.astype(BF16))
    triple_low, p0, p1, p2, p3, triple_sums = vmem_call(
        partial(attend_back_kernel, factor),
        [array((length, 3 * width))] + [rows_out] * MP + [array((1, 3 * width), F32)],
        8 * 10**9,
        triple,
        turned_low,
        log_totals,
        *mixed_grads,
        first_all,
        scratch=[pltpu.VMEM((length, 3 * width), F32)],
        limit=22,
    )
    parts = [p0] + [shift_mp(p, MP - k) for k, p in ((1, p1), (2, p2), (3, p3))]
    local_sums = jnp.concatenate(
        [
            triple_sums[:, :width],
            triple_sums[:, 2 * width :],
            inner_total.reshape(width, MP).T,
        ]
    )
    triple_low, feed_total = lax.optimization_barrier((triple_low, feed_total))
    feed_sums = jnp.sum(feed_total.astype(F32), axis=0)
    blocks = array((PLANE, depth, 4 * width + vectors))
    last_mine, last_other = vmem_call(
        last_grad_kernel,
        [blocks, blocks],
        10**9,
        core_index,
        position_index,
        normed,
        triple_low,
        first_all,
        *out_grads,
        first_norms,
        middle_sums,
        local_sums,
        scratch=[pltpu.VMEM((model, 4 * width + vectors), F32)],
        limit=16,
    )
    last_total = last_mine.astype(F32) + swap_cores(last_other).astype(F32)
    last_total = exchange_plane(last_total.astype(BF16))
    last_total, *parts = lax.optimization_barrier((last_total, *parts))
    last_sums = jnp.sum(last_total.astype(F32), axis=0)
    tail = last_sums[:, 4 * width :]
    tail = tail + sum(shift_mp(tail, k) for k in range(1, MP))
    pieces = lax.dynamic_slice_in_dim(tail, position * each, each, axis=0)
    inner_piece = pieces[:, 8:].reshape(MP * each)
    (frames_grad,) = vmem_call(
        rows_back_kernel,
        [rows_out],
        10**8,
        *parts,
        frames[0],
        first_norms[0:1],
        middle_grad,
        limit=8,
    )
    return (
        output,
        frames_grad[None],
        pieces[:, 0],
        pieces[:, 1],
        last_sums[:, :width],
        pieces[:, 6],
        last_sums[:, width : 2 * width],
        last_sums[:, 2 * width : 3 * width],
        pieces[:, 7],
        last_sums[:, 3 * width : 4 * width].T,
        pieces[:, 2],
        pieces[:, 3],
        pieces[:, 4],
        feed_sums[:, :hidden],
        inner_piece,
        feed_sums[:, hidden:].T,
        pieces[:, 5],
    )


def solution(mesh):
    mesh = Mesh(mesh.devices.reshape(PLANE, CORES, MP), ("yz", "core", "mp"))
    rows = P(("yz", "core"), "mp", None)
    vector = P(("yz", "core", "mp"))
    wide = P(("yz", "core"), "mp")
    tall = P("mp", ("yz", "core"))
    in_specs = (
        rows, vector, vector, wide, vector, wide, wide, vector, tall, vector,
        vector, vector, wide, vector, tall, vector, rows,
    )
    out_specs = (
        rows, rows, vector, vector, wide, vector, wide, wide, vector, tall,
        vector, vector, vector, wide, vector, tall, vector,
    )
    return jax.shard_map(shards, mesh=mesh, in_specs=in_specs, out_specs=out_specs, check_vma=False)
```

```python
from functools import partial

import jax
import jax.numpy as jnp
import numpy as np
from jax import lax
from jax.experimental import pallas as pl
from jax.experimental.pallas import tpu as pltpu
from jax.sharding import Mesh
from jax.sharding import PartitionSpec as P

HD = 64
MP = 4
PLANE = 16
CORES = 2
EPS = 1e-05

F32 = jnp.float32
BF16 = jnp.bfloat16


def shift_mp(piece, step):
    return lax.ppermute(piece, "mp", [(i, (i + step) % MP) for i in range(MP)])


def spread_rows(rows):
    return [rows] + [shift_mp(rows, k) for k in range(1, MP)]


def swap_cores(piece):
    return lax.ppermute(piece, "core", [(0, 1), (1, 0)])


def exchange_plane(blocks):
    return lax.all_to_all(blocks, "yz", 0, 0, tiled=True)


def join_cores(found, other, core):
    both = jnp.stack(
        [jnp.where(core == 0, found, other), jnp.where(core == 0, other, found)], axis=1
    )
    return both.reshape(2 * found.shape[0] * found.shape[1], found.shape[2])


def turn_over(matrix):
    unit = jnp.eye(matrix.shape[1], dtype=BF16)
    return lax.dot_general(unit, matrix, (((1,), (1,)), ((), ())), preferred_element_type=F32)


def gelu_parts(inner):
    density = jnp.exp(-0.5 * inner * inner)
    size = jnp.abs(inner) * (0.5**0.5)
    t = 1.0 / (1.0 + 0.3275911 * size)
    poly = 1.061405429
    for term in (-1.453152027, 1.421413741, -0.284496736, 0.254829592):
        poly = poly * t + term
    tail = 0.5 * poly * t * density
    return (jnp.where(inner < 0, tail, 1.0 - tail), density * 0.3989422804014327)


def vmem_call(kernel, outs, flops, *operands, scratch=(), limit=20):
    size = sum(a.size * a.dtype.itemsize for a in operands) + sum(
        o.size * o.dtype.itemsize for o in outs
    )
    return pl.pallas_call(
        kernel,
        out_shape=tuple(outs),
        in_specs=[
            pl.BlockSpec(memory_space=pltpu.SMEM if a.dtype == jnp.int32 else pltpu.VMEM)
            for a in operands
        ],
        out_specs=tuple(pl.BlockSpec(memory_space=pltpu.VMEM) for _ in outs),
        scratch_shapes=list(scratch),
        compiler_params=pltpu.CompilerParams(vmem_limit_bytes=limit * 2**20),
        cost_estimate=pl.CostEstimate(flops=flops, bytes_accessed=size, transcendentals=0),
    )(*operands)


def array(shape, dtype=BF16):
    return jax.ShapeDtypeStruct(shape, dtype)


def dot(left, right, sides=(1, 0)):
    return lax.dot_general(
        left, right, (((sides[0],), (sides[1],)), ((), ())), preferred_element_type=F32
    )


def split_cores(total, core, mine, other, columns=slice(None)):
    depth = mine.shape[1]
    for i in range(mine.shape[0]):
        start = pl.multiple_of((2 * i + core[0]) * depth, 8)
        mine[i, :, columns] = total[pl.ds(start, depth), :].astype(BF16)
        start = pl.multiple_of((2 * i + 1 - core[0]) * depth, 8)
        other[i, :, columns] = total[pl.ds(start, depth), :].astype(BF16)


def scaled_rows(rows):
    centred = rows - jnp.mean(rows, axis=-1, keepdims=True)
    inverse = lax.rsqrt(jnp.mean(centred * centred, axis=-1, keepdims=True) + EPS)
    return (centred * inverse, inverse)


def first_pack_kernel(c0, c1, c2, c3, query, key, value, out):
    width = query.shape[1]
    pieces = [c[:, :width] for c in (c0, c1, c2, c3)] + [query[...], key[...], value[...]]
    for i, piece in enumerate(pieces):
        for k in range(out.shape[0]):
            out[k, :, i * width : (i + 1) * width] = piece
    vectors = c0[:, width:].astype(F32)
    for c in (c1, c2, c3):
        vectors = vectors + c[:, width:].astype(F32)
    for k in range(out.shape[0]):
        out[k, :, len(pieces) * width :] = vectors.astype(BF16)


def feed_pack_kernel(inner, turned_outer, out):
    out[:, : inner.shape[1]] = inner[...]
    out[:, inner.shape[1] :] = turned_outer[...]


def slot_rows(position, k, rows):
    return pl.ds(pl.multiple_of(lax.rem(position[0] + MP - k, MP) * rows, rows), rows)


def attend_kernel(factor, position, raw, weight, norms, offset, normed, triple, turned_low, m0, m1, m2, m3, log_totals):
    rows, length = m0.shape[0], normed.shape[0]
    width = m0.shape[1]
    for k in range(MP):
        scaled, _ = scaled_rows(raw[slot_rows(position, k, rows), :].astype(F32))
        low = (scaled * norms[0:1, :] + norms[1:2, :]).astype(BF16)
        normed[k * rows : (k + 1) * rows, :] = low
        projected = dot(low, weight[:, 4 * width : 7 * width]) + offset[...]
        triple[k * rows : (k + 1) * rows, :] = projected.astype(BF16)
        turned_low[:, k * rows : (k + 1) * rows] = projected.T.astype(BF16)
    for h in range(width // HD):
        keys = triple[:, width + h * HD : width + (h + 1) * HD]
        values = turned_low[2 * width + h * HD : 2 * width + (h + 1) * HD, :]
        for k, mixed in enumerate((m0, m1, m2, m3)):
            block = slice(k * rows, (k + 1) * rows)
            queries = turned_low[h * HD : (h + 1) * HD, block] * factor
            scores = dot(keys, queries)
            highest = jnp.max(scores, axis=0, keepdims=True)
            expd = jnp.exp(scores - highest)
            totals = jnp.sum(expd, axis=0, keepdims=True)
            found = dot(values, expd.astype(BF16)) / totals
            mixed[:, h * HD : (h + 1) * HD] = found.T.astype(BF16)
            log_totals[h : h + 1, block] = highest + jnp.log(totals)


def attend_back_kernel(
    factor, core, position, triple, turned_low, log_totals, g0, g1, g2, g3, weight,
    normed, norms, middle_sums, inner_sums, p0, p1, p2, p3, mine, other, total, grads,
):
    rows, width = g0.shape
    model = weight.shape[0]
    third = 3 * width
    turned_grads = [g[...].astype(F32).T.astype(BF16) for g in (g0, g1, g2, g3)]
    for h in range(width // HD):
        head = slice(h * HD, (h + 1) * HD)
        keys = triple[:, width + h * HD : width + (h + 1) * HD]
        values = triple[:, 2 * width + h * HD : 2 * width + (h + 1) * HD]
        turned_keys = turned_low[width + h * HD : width + (h + 1) * HD, :]
        key_grad, value_grad = 0.0, 0.0
        for k, g in enumerate((g0, g1, g2, g3)):
            block = slice(k * rows, (k + 1) * rows)
            scores = dot(keys, turned_low[head, block] * factor)
            probs = jnp.exp(scores - log_totals[h : h + 1, block])
            prob_grad = dot(values, turned_grads[k][head, :])
            inside = jnp.sum(probs * prob_grad, axis=0, keepdims=True)
            score_grad = (probs * (prob_grad - inside)).astype(BF16)
            value_grad = value_grad + dot(probs.astype(BF16), g[:, head])
            key_grad = key_grad + dot(score_grad, triple[block, head])
            total[block, head] = (dot(turned_keys, score_grad) * float(factor)).T
        total[:, width + h * HD : width + (h + 1) * HD] = key_grad * float(factor)
        total[:, 2 * width + h * HD : 2 * width + (h + 1) * HD] = value_grad
    low = total[...].astype(BF16)
    for k, p in enumerate((p0, p1, p2, p3)):
        part = low[k * rows : (k + 1) * rows, :]
        p[...] = dot(part, weight[:, model : model + third], (1, 1)).astype(BF16)
    found = dot(normed[...].astype(F32).T.astype(BF16), low)
    grads[:, :third] = found
    wide = weight[:, model : model + third].astype(F32)
    row_sum = jnp.sum(low.astype(F32), axis=0, keepdims=True)
    shift_grad = jnp.sum(wide * row_sum, axis=1, keepdims=True)
    gain_grad = jnp.sum(wide * found, axis=1, keepdims=True)
    turned_norms = norms[...].T
    gain_grad = (gain_grad - turned_norms[:, 1:2] * shift_grad) / turned_norms[:, 0:1]
    grads[:, third:] = jnp.zeros((model, grads.shape[1] - third), F32)
    grads[:, third : third + 1] = gain_grad
    grads[:, third + 1 : third + 2] = shift_grad
    grads[:, third + 2 : third + 6] = middle_sums[...].T
    bias_sum = jnp.sum(total[...], axis=0, keepdims=True)
    row = pl.multiple_of(position[0] * width, 8)
    grads[pl.ds(row, width), third + 6 : third + 7] = bias_sum[:, :width].T
    grads[pl.ds(row, width), third + 7 : third + 8] = bias_sum[:, 2 * width :].T
    grads[pl.ds(row, width), third + 8 : third + 12] = inner_sums[...]
    split_cores(grads, core, mine, other)


def middle_kernel(m0, m1, m2, m3, weight, source, norms, middle, normed):
    total = source[...].astype(F32) + norms[2:3, :]
    width = m0.shape[1]
    for k, m in enumerate((m0, m1, m2, m3)):
        total = total + dot(m[...], weight[:, k * width : (k + 1) * width], (1, 1))
    middle[...] = total
    scaled, _ = scaled_rows(total)
    normed[...] = (scaled * norms[0:1, :] + norms[1:2, :]).astype(BF16)


def feed_kernel(k, last, position, core, normed, up, weights, offset, *refs):
    if k > 0:
        grads_in, fed_in, sums_in, *refs = refs
    if last:
        second, mine, other, fed, sums, grads = refs
    else:
        second, grads, fed, sums = refs
    rows = normed.shape[0]
    hidden = weights.shape[1] // 2
    inner = dot(normed[...], weights[:, :hidden]) + offset[...]
    whole, density = gelu_parts(inner)
    active = (inner * whole).astype(BF16)
    grad = dot(up[...], weights[:, hidden:]) * (whole + inner * density)
    low = grad.astype(BF16)
    second[...] = dot(low, weights[:, :hidden], (1, 1)).astype(BF16)
    sum_here = jnp.sum(grad, axis=0, keepdims=True)
    turned_normed = normed[...].astype(F32).T.astype(BF16)
    turned_up = up[...].astype(F32).T.astype(BF16)
    if k > 0:
        fed[...] = fed_in[...]
        sums[...] = sums_in[...] + sum_here
        grads[:, :hidden] = grads_in[:, :hidden] + dot(turned_normed, low)
        grads[:, hidden:] = grads_in[:, hidden:] + dot(turned_up, active)
    else:
        sums[...] = sum_here
        grads[:, :hidden] = dot(turned_normed, low)
        grads[:, hidden:] = dot(turned_up, active)
    fed[slot_rows(position, k, rows), :] = dot(active, weights[:, hidden:], (1, 1)).astype(BF16)
    if last:
        split_cores(grads, core, mine, other)


def middle_back_kernel(
    core, s0, s1, s2, s3, middle, up, norms, weight, m0, m1, m2, m3,
    middle_grad, h0, h1, h2, h3, mine, other, sums, grads,
):
    grad = s0[...].astype(F32)
    for s in (s1, s2, s3):
        grad = grad + s[...].astype(F32)
    scaled, inverse = scaled_rows(middle[...])
    weighted = grad * norms[0:1, :]
    upstream = up[...].astype(F32)
    total = upstream + inverse * (
        weighted
        - jnp.mean(weighted, axis=-1, keepdims=True)
        - scaled * jnp.mean(weighted * scaled, axis=-1, keepdims=True)
    )
    middle_grad[...] = total
    low = total.astype(BF16)
    turned = total.T.astype(BF16)
    for k, m in enumerate((m0, m1, m2, m3)):
        grads[:, k * m.shape[1] : (k + 1) * m.shape[1]] = dot(turned, m[...])
    split_cores(grads, core, mine, other)
    width = h0.shape[1]
    for k, h in enumerate((h0, h1, h2, h3)):
        h[...] = dot(low, weight[:, k * width : (k + 1) * width]).astype(BF16)
    sums[0:1, :] = jnp.sum(total, axis=0, keepdims=True)
    sums[1:2, :] = jnp.sum(grad * scaled, axis=0, keepdims=True)
    sums[2:3, :] = jnp.sum(grad, axis=0, keepdims=True)
    sums[3:4, :] = jnp.sum(upstream, axis=0, keepdims=True)


def join_kernel(f, f_received, o, o_received, total):
    columns = f.shape[2]
    for i in range(f.shape[0]):
        total[i, :, :columns] = (f[i].astype(F32) + f_received[i].astype(F32)).astype(BF16)
        total[i, :, columns:] = (o[i].astype(F32) + o_received[i].astype(F32)).astype(BF16)


def rows_back_kernel(p0, p1, p2, p3, source, gain, middle_grad, out):
    grad = p0[...].astype(F32)
    for p in (p1, p2, p3):
        grad = grad + p[...].astype(F32)
    scaled, inverse = scaled_rows(source[...].astype(F32))
    weighted = grad * gain[...]
    back = inverse * (
        weighted
        - jnp.mean(weighted, axis=-1, keepdims=True)
        - scaled * jnp.mean(weighted * scaled, axis=-1, keepdims=True)
    )
    out[...] = (middle_grad[...] + back).astype(BF16)


def shards(
    frames,
    attend_gain,
    attend_shift,
    query_weight,
    query_bias,
    key_weight,
    value_weight,
    value_bias,
    out_weight,
    out_bias,
    feed_gain,
    feed_shift,
    inner_weight,
    inner_bias,
    outer_weight,
    outer_bias,
    cotangent,
):
    position = lax.axis_index("mp")
    core = lax.axis_index("core")
    rows = frames.shape[1]
    length = rows * MP
    model = frames.shape[2]
    width = query_weight.shape[1]
    hidden = inner_weight.shape[1]
    depth = query_weight.shape[0]
    each = attend_gain.shape[0]
    heads = width // HD
    factor = HD ** (-0.5)
    slots = range(MP)
    core_index = core.reshape(1)
    position_index = position.reshape(1)

    vectors = 8 + MP
    pieces = (
        attend_gain,
        attend_shift,
        query_bias,
        value_bias,
        out_bias,
        feed_gain,
        feed_shift,
        outer_bias,
        inner_bias,
    )
    packed = sum(
        jnp.pad(v.astype(F32), (i * each, (8 + MP) * each - i * each - v.shape[0]))
        for i, v in enumerate(pieces)
    )
    entry = np.arange(vectors * each)
    early = entry < 8 * each
    row_of = np.where(early, entry % each, (entry - 8 * each) // MP)
    column_of = np.where(early, entry // each, 8 + (entry - 8 * each) % MP)
    to_column = jnp.asarray(column_of[:, None] == np.arange(vectors)[None], BF16)
    at_row = lax.iota(jnp.int32, depth)[:, None] == position * each + jnp.asarray(row_of, jnp.int32)
    piece = dot(jnp.where(at_row, packed[None], 0).astype(BF16), to_column).astype(BF16)
    carried = jnp.concatenate([turn_over(out_weight).astype(BF16), piece], axis=1)
    carried = [carried] + [shift_mp(carried, MP - k) for k in range(1, MP)]
    full_raw = lax.all_gather(frames[0], "mp", axis=0, tiled=True)
    (first_blocks,) = vmem_call(
        first_pack_kernel,
        [array((PLANE, depth, model + 3 * width + vectors))],
        10**6,
        *carried,
        query_weight,
        key_weight,
        value_weight,
        limit=52,
    )
    found = exchange_plane(first_blocks)
    inner_weight, outer_weight, found = lax.optimization_barrier(
        (inner_weight, outer_weight, found)
    )
    (feed_block,) = vmem_call(
        feed_pack_kernel, [array((depth, 2 * hidden))], 10**6, inner_weight, outer_weight.T, limit=4
    )
    feed_all = lax.all_gather(feed_block, ("yz", "core"), axis=0, tiled=True)
    first_all = join_cores(found, swap_cores(found), core)
    small = first_all[:, model + 3 * width :].T.astype(F32)
    first_norms = small[0:2]
    second_norms = jnp.stack([small[5], small[6], small[4]])
    local = lax.dynamic_slice_in_dim(small, position * width, width, axis=1)
    offset = jnp.concatenate([local[2], jnp.zeros_like(local[2]), local[3]])[None]
    inner_offset = local[8:].T.reshape(1, MP * width)

    rows_out = array((rows, model))
    heads_out = array((rows, width))
    normed, triple, turned_low, m0, m1, m2, m3, log_totals = vmem_call(
        partial(attend_kernel, factor),
        [
            array((length, model)),
            array((length, 3 * width)),
            array((3 * width, length)),
            heads_out,
            heads_out,
            heads_out,
            heads_out,
            array((heads, length), F32),
        ],
        4 * 10**9,
        position_index,
        full_raw,
        first_all,
        first_norms,
        offset,
        limit=18,
    )
    upstream_low = cotangent[0]
    ups = spread_rows(upstream_low)
    m1, m2, m3, *ups = lax.optimization_barrier((m1, m2, m3, *ups))
    own_mixed = [m0] + [shift_mp(m, MP - k) for k, m in ((1, m1), (2, m2), (3, m3))]
    own_mixed = list(lax.optimization_barrier(tuple(own_mixed)))
    middle, normed_two = vmem_call(
        middle_kernel,
        [array((rows, model), F32), rows_out],
        10**9,
        *own_mixed,
        first_all,
        frames[0],
        second_norms,
        limit=10,
    )
    twos = [normed_two, shift_mp(normed_two, 1), None, shift_mp(normed_two, MP - 1)]
    seconds, carry = {}, ()
    inner_sums = array((1, hidden), F32)
    feed_blocks = array((PLANE, depth, 2 * hidden))
    for k in (0, 1, 3, 2):
        last = k == 2
        grads = array((model, 2 * hidden), F32)
        fed_out = array((length, model))
        outs = [rows_out, feed_blocks, feed_blocks, fed_out, inner_sums]
        found = vmem_call(
            partial(feed_kernel, k, last),
            outs if last else [rows_out, grads, fed_out, inner_sums],
            5 * 10**9,
            position_index,
            core_index,
            twos[k],
            ups[k],
            feed_all,
            inner_offset,
            *carry,
            scratch=[pltpu.VMEM(grads.shape, F32)] if last else [],
            limit=16,
        )
        seconds[k] = found[0]
        if last:
            feed_mine, feed_other, fed_all, inner_total = found[1:]
        else:
            carry = found[1:]
        if k == 0:
            twos[1], twos[3], _ = lax.optimization_barrier((twos[1], twos[3], carry[2]))
            far = (shift_mp(twos[1][: rows // 2], 1), shift_mp(twos[3][rows // 2 :], MP - 1))
        if k == 3:
            *far, _ = lax.optimization_barrier((*far, carry[2]))
            twos[2] = jnp.concatenate(far)
    seconds = [seconds[0]] + [shift_mp(seconds[k], MP - k) for k in range(1, MP)]
    feed_mine, feed_other, seconds[1], seconds[3] = lax.optimization_barrier(
        (feed_mine, feed_other, seconds[1], seconds[3])
    )
    feed_total = feed_mine.astype(F32) + swap_cores(feed_other).astype(F32)
    feed_total = feed_total.astype(BF16)
    feed_total, seconds[2] = lax.optimization_barrier((feed_total, seconds[2]))
    feed_total = exchange_plane(feed_total)
    out_blocks = array((PLANE, depth, model))
    middle_grad, h0, h1, h2, h3, out_mine, out_other, middle_sums = vmem_call(
        middle_back_kernel,
        [
            array((rows, model), F32),
            *[heads_out] * MP,
            out_blocks,
            out_blocks,
            array((4, model), F32),
        ],
        10**9,
        core_index,
        *seconds,
        middle,
        upstream_low,
        second_norms,
        first_all,
        *own_mixed,
        scratch=[pltpu.VMEM((model, model), F32)],
        limit=52,
    )
    mixed_grads = [h0] + [shift_mp(h, k) for k, h in ((1, h1), (2, h2), (3, h3))]
    fed_all, *mixed_grads = lax.optimization_barrier((fed_all, *mixed_grads))
    fed = lax.psum_scatter(fed_all, "mp", scatter_dimension=0, tiled=True)
    out_other, h1 = lax.optimization_barrier((out_other, h1))
    out_received = swap_cores(out_other)
    blocks = array((PLANE, depth, 3 * width + vectors))
    *parts, last_mine, last_other = vmem_call(
        partial(attend_back_kernel, factor),
        [rows_out] * MP + [blocks, blocks],
        8 * 10**9,
        core_index,
        position_index,
        triple,
        turned_low,
        log_totals,
        *mixed_grads,
        first_all,
        normed,
        first_norms,
        middle_sums,
        inner_total.reshape(width, MP),
        scratch=[
            pltpu.VMEM((length, 3 * width), F32),
            pltpu.VMEM((model, 3 * width + vectors), F32),
        ],
        limit=52,
    )
    last_mine, last_other, feed_total, out_received = lax.optimization_barrier(
        (last_mine, last_other, feed_total, out_received)
    )
    last_received = swap_cores(last_other)
    parts = [parts[0]] + [shift_mp(parts[k], MP - k) for k in range(1, MP)]
    (last_total,) = vmem_call(
        join_kernel,
        [array((PLANE, depth, 3 * width + vectors + model))],
        10**6,
        out_mine,
        out_received,
        last_mine,
        last_received,
        limit=14,
    )
    last_total = exchange_plane(last_total)
    last_total, fed, *parts = lax.optimization_barrier((last_total, fed, *parts))
    output = middle + small[7] + fed.astype(F32)
    output = output.astype(BF16)[None]
    feed_sums = jnp.sum(feed_total.astype(F32), axis=0)
    last_sums = jnp.sum(last_total.astype(F32), axis=0)
    tails = [
        jnp.concatenate(
            [
                last_sums[:, model + 3 * width :],
                last_sums[:, k * width : (k + 1) * width],
            ],
            axis=1,
        )
        for k in slots
    ]
    tail = tails[0] + sum(shift_mp(tails[k], k) for k in range(1, MP))
    pieces = lax.dynamic_slice_in_dim(tail, position * each, each, axis=0)
    inner_piece = pieces[:, 8:vectors].reshape(MP * each)
    (frames_grad,) = vmem_call(
        rows_back_kernel,
        [rows_out],
        10**8,
        *parts,
        frames[0],
        first_norms[0:1],
        middle_grad,
        limit=8,
    )
    return (
        output,
        frames_grad[None],
        pieces[:, 0],
        pieces[:, 1],
        last_sums[:, model : model + width],
        pieces[:, 6],
        last_sums[:, model + width : model + 2 * width],
        last_sums[:, model + 2 * width : model + 3 * width],
        pieces[:, 7],
        tail[:, vectors:].T,
        pieces[:, 2],
        pieces[:, 3],
        pieces[:, 4],
        feed_sums[:, :hidden],
        inner_piece,
        feed_sums[:, hidden : 2 * hidden].T,
        pieces[:, 5],
    )


def solution(mesh):
    mesh = Mesh(mesh.devices.reshape(PLANE, CORES, MP), ("yz", "core", "mp"))
    rows = P(("yz", "core"), "mp", None)
    vector = P(("yz", "core", "mp"))
    wide = P(("yz", "core"), "mp")
    tall = P("mp", ("yz", "core"))
    in_specs = (
        rows, vector, vector, wide, vector, wide, wide, vector, tall, vector,
        vector, vector, wide, vector, tall, vector, rows,
    )
    out_specs = (
        rows, rows, vector, vector, wide, vector, wide, wide, vector, tall,
        vector, vector, vector, wide, vector, tall, vector,
    )
    return jax.shard_map(shards, mesh=mesh, in_specs=in_specs, out_specs=out_specs, check_vma=False)
```

```python
from functools import partial

import jax
import jax.numpy as jnp
import numpy as np
from jax import lax
from jax.experimental import pallas as pl
from jax.experimental.pallas import tpu as pltpu
from jax.sharding import Mesh
from jax.sharding import PartitionSpec as P

HD = 64
MP = 4
PLANE = 16
CORES = 2
EPS = 1e-05

F32 = jnp.float32
BF16 = jnp.bfloat16


def shift_mp(piece, step):
    return lax.ppermute(piece, "mp", [(i, (i + step) % MP) for i in range(MP)])


def spread_rows(rows):
    return [rows] + [shift_mp(rows, k) for k in range(1, MP)]


def swap_cores(piece):
    return lax.ppermute(piece, "core", [(0, 1), (1, 0)])


def exchange_plane(blocks):
    return lax.all_to_all(blocks, "yz", 0, 0, tiled=True)


def join_cores(found, other, core):
    both = jnp.stack(
        [jnp.where(core == 0, found, other), jnp.where(core == 0, other, found)], axis=1
    )
    return both.reshape(2 * found.shape[0] * found.shape[1], found.shape[2])


def turn_over(matrix):
    unit = jnp.eye(matrix.shape[1], dtype=BF16)
    return lax.dot_general(unit, matrix, (((1,), (1,)), ((), ())), preferred_element_type=F32)


def gelu_parts(inner):
    density = jnp.exp(-0.5 * inner * inner)
    size = jnp.abs(inner) * (0.5**0.5)
    t = 1.0 / (1.0 + 0.3275911 * size)
    poly = 1.061405429
    for term in (-1.453152027, 1.421413741, -0.284496736, 0.254829592):
        poly = poly * t + term
    tail = 0.5 * poly * t * density
    return (jnp.where(inner < 0, tail, 1.0 - tail), density * 0.3989422804014327)


def vmem_call(kernel, outs, flops, *operands, scratch=(), limit=20):
    size = sum(a.size * a.dtype.itemsize for a in operands) + sum(
        o.size * o.dtype.itemsize for o in outs
    )
    return pl.pallas_call(
        kernel,
        out_shape=tuple(outs),
        in_specs=[
            pl.BlockSpec(memory_space=pltpu.SMEM if a.dtype == jnp.int32 else pltpu.VMEM)
            for a in operands
        ],
        out_specs=tuple(pl.BlockSpec(memory_space=pltpu.VMEM) for _ in outs),
        scratch_shapes=list(scratch),
        compiler_params=pltpu.CompilerParams(vmem_limit_bytes=limit * 2**20),
        cost_estimate=pl.CostEstimate(flops=flops, bytes_accessed=size, transcendentals=0),
    )(*operands)


def array(shape, dtype=BF16):
    return jax.ShapeDtypeStruct(shape, dtype)


def dot(left, right, sides=(1, 0)):
    return lax.dot_general(
        left, right, (((sides[0],), (sides[1],)), ((), ())), preferred_element_type=F32
    )


def split_cores(total, core, mine, other, columns=slice(None)):
    depth = mine.shape[1]
    for i in range(mine.shape[0]):
        start = pl.multiple_of((2 * i + core[0]) * depth, 8)
        mine[i, :, columns] = total[pl.ds(start, depth), :].astype(BF16)
        start = pl.multiple_of((2 * i + 1 - core[0]) * depth, 8)
        other[i, :, columns] = total[pl.ds(start, depth), :].astype(BF16)


def scaled_rows(rows):
    centred = rows - jnp.mean(rows, axis=-1, keepdims=True)
    inverse = lax.rsqrt(jnp.mean(centred * centred, axis=-1, keepdims=True) + EPS)
    return (centred * inverse, inverse)


def first_pack_kernel(c0, c1, c2, c3, query, key, value, out):
    width = query.shape[1]
    pieces = [c[:, :width] for c in (c0, c1, c2, c3)] + [query[...], key[...], value[...]]
    for i, piece in enumerate(pieces):
        for k in range(out.shape[0]):
            out[k, :, i * width : (i + 1) * width] = piece
    vectors = c0[:, width:].astype(F32)
    for c in (c1, c2, c3):
        vectors = vectors + c[:, width:].astype(F32)
    for k in range(out.shape[0]):
        out[k, :, len(pieces) * width :] = vectors.astype(BF16)


def feed_pack_kernel(inner, turned_outer, out):
    out[:, : inner.shape[1]] = inner[...]
    out[:, inner.shape[1] :] = turned_outer[...]


def slot_rows(position, k, rows):
    return pl.ds(pl.multiple_of(lax.rem(position[0] + MP - k, MP) * rows, rows), rows)


def attend_kernel(factor, position, raw, weight, norms, offset, normed, triple, turned_low, m0, m1, m2, m3, log_totals, kept):
    rows, length = m0.shape[0], normed.shape[0]
    width = m0.shape[1]
    for k in range(MP):
        scaled, _ = scaled_rows(raw[slot_rows(position, k, rows), :].astype(F32))
        low = (scaled * norms[0:1, :] + norms[1:2, :]).astype(BF16)
        normed[k * rows : (k + 1) * rows, :] = low
        projected = dot(low, weight[:, 4 * width : 7 * width]) + offset[...]
        triple[k * rows : (k + 1) * rows, :] = projected.astype(BF16)
        turned_low[:, k * rows : (k + 1) * rows] = projected.T.astype(BF16)
    for h in range(width // HD):
        keys = triple[:, width + h * HD : width + (h + 1) * HD]
        values = turned_low[2 * width + h * HD : 2 * width + (h + 1) * HD, :]
        for k, mixed in enumerate((m0, m1, m2, m3)):
            block = slice(k * rows, (k + 1) * rows)
            queries = turned_low[h * HD : (h + 1) * HD, block] * factor
            scores = dot(keys, queries)
            highest = jnp.max(scores, axis=0, keepdims=True)
            expd = jnp.exp(scores - highest)
            totals = jnp.sum(expd, axis=0, keepdims=True)
            found = dot(values, expd.astype(BF16)) / totals
            mixed[:, h * HD : (h + 1) * HD] = found.T.astype(BF16)
            kept[h * HD : (h + 1) * HD, block] = found
            log_totals[h : h + 1, block] = highest + jnp.log(totals)


def attend_back_kernel(
    factor, core, position, triple, turned_low, log_totals, kept, g0, g1, g2, g3, weight,
    normed, norms, middle_sums, inner_sums, p0, p1, p2, p3, mine, other, total, grads,
):
    rows, width = g0.shape
    model = weight.shape[0]
    third = 3 * width
    turned_grads = [g[...].astype(F32).T.astype(BF16) for g in (g0, g1, g2, g3)]
    for h in range(width // HD):
        head = slice(h * HD, (h + 1) * HD)
        keys = triple[:, width + h * HD : width + (h + 1) * HD]
        values = triple[:, 2 * width + h * HD : 2 * width + (h + 1) * HD]
        turned_keys = turned_low[width + h * HD : width + (h + 1) * HD, :]
        key_grad, value_grad = 0.0, 0.0
        for k, g in enumerate((g0, g1, g2, g3)):
            block = slice(k * rows, (k + 1) * rows)
            scores = dot(keys, turned_low[head, block] * factor)
            probs = jnp.exp(scores - log_totals[h : h + 1, block])
            prob_grad = dot(values, turned_grads[k][head, :])
            inside = jnp.sum(
                kept[head, block] * turned_grads[k][head, :].astype(F32), axis=0, keepdims=True
            )
            score_grad = (probs * (prob_grad - inside)).astype(BF16)
            value_grad = value_grad + dot(probs.astype(BF16), g[:, head])
            key_grad = key_grad + dot(score_grad, triple[block, head])
            total[block, head] = (dot(turned_keys, score_grad) * float(factor)).T
        total[:, width + h * HD : width + (h + 1) * HD] = key_grad * float(factor)
        total[:, 2 * width + h * HD : 2 * width + (h + 1) * HD] = value_grad
    low = total[...].astype(BF16)
    for k, p in enumerate((p0, p1, p2, p3)):
        part = low[k * rows : (k + 1) * rows, :]
        p[...] = dot(part, weight[:, model : model + third], (1, 1)).astype(BF16)
    found = dot(normed[...].astype(F32).T.astype(BF16), low)
    grads[:, :third] = found
    wide = weight[:, model : model + third].astype(F32)
    row_sum = jnp.sum(low.astype(F32), axis=0, keepdims=True)
    shift_grad = jnp.sum(wide * row_sum, axis=1, keepdims=True)
    gain_grad = jnp.sum(wide * found, axis=1, keepdims=True)
    turned_norms = norms[...].T
    gain_grad = (gain_grad - turned_norms[:, 1:2] * shift_grad) / turned_norms[:, 0:1]
    grads[:, third:] = jnp.zeros((model, grads.shape[1] - third), F32)
    grads[:, third : third + 1] = gain_grad
    grads[:, third + 1 : third + 2] = shift_grad
    grads[:, third + 2 : third + 6] = middle_sums[...].T
    bias_sum = jnp.sum(total[...], axis=0, keepdims=True)
    row = pl.multiple_of(position[0] * width, 8)
    grads[pl.ds(row, width), third + 6 : third + 7] = bias_sum[:, :width].T
    grads[pl.ds(row, width), third + 7 : third + 8] = bias_sum[:, 2 * width :].T
    grads[pl.ds(row, width), third + 8 : third + 12] = inner_sums[...]
    split_cores(grads, core, mine, other)


def middle_kernel(m0, m1, m2, m3, weight, source, norms, middle, normed):
    total = source[...].astype(F32) + norms[2:3, :]
    width = m0.shape[1]
    for k, m in enumerate((m0, m1, m2, m3)):
        total = total + dot(m[...], weight[:, k * width : (k + 1) * width], (1, 1))
    middle[...] = total
    scaled, _ = scaled_rows(total)
    normed[...] = (scaled * norms[0:1, :] + norms[1:2, :]).astype(BF16)


def feed_kernel(k, last, position, core, normed, up, weights, offset, *refs):
    if k > 0:
        grads_in, fed_in, sums_in, *refs = refs
    if last:
        second, mine, other, fed, sums, grads = refs
    else:
        second, grads, fed, sums = refs
    rows = normed.shape[0]
    hidden = weights.shape[1] // 2
    inner = dot(normed[...], weights[:, :hidden]) + offset[...]
    whole, density = gelu_parts(inner)
    active = (inner * whole).astype(BF16)
    grad = dot(up[...], weights[:, hidden:]) * (whole + inner * density)
    low = grad.astype(BF16)
    second[...] = dot(low, weights[:, :hidden], (1, 1)).astype(BF16)
    sum_here = jnp.sum(grad, axis=0, keepdims=True)
    turned_normed = normed[...].astype(F32).T.astype(BF16)
    turned_up = up[...].astype(F32).T.astype(BF16)
    if k > 0:
        fed[...] = fed_in[...]
        sums[...] = sums_in[...] + sum_here
        grads[:, :hidden] = grads_in[:, :hidden] + dot(turned_normed, low)
        grads[:, hidden:] = grads_in[:, hidden:] + dot(turned_up, active)
    else:
        sums[...] = sum_here
        grads[:, :hidden] = dot(turned_normed, low)
        grads[:, hidden:] = dot(turned_up, active)
    fed[slot_rows(position, k, rows), :] = dot(active, weights[:, hidden:], (1, 1)).astype(BF16)
    if last:
        split_cores(grads, core, mine, other)


def middle_back_kernel(
    core, s0, s1, s2, s3, middle, up, norms, weight, m0, m1, m2, m3,
    middle_grad, h0, h1, h2, h3, mine, other, sums, grads,
):
    grad = s0[...].astype(F32)
    for s in (s1, s2, s3):
        grad = grad + s[...].astype(F32)
    scaled, inverse = scaled_rows(middle[...])
    weighted = grad * norms[0:1, :]
    upstream = up[...].astype(F32)
    total = upstream + inverse * (
        weighted
        - jnp.mean(weighted, axis=-1, keepdims=True)
        - scaled * jnp.mean(weighted * scaled, axis=-1, keepdims=True)
    )
    middle_grad[...] = total
    low = total.astype(BF16)
    turned = total.T.astype(BF16)
    for k, m in enumerate((m0, m1, m2, m3)):
        grads[:, k * m.shape[1] : (k + 1) * m.shape[1]] = dot(turned, m[...])
    split_cores(grads, core, mine, other)
    width = h0.shape[1]
    for k, h in enumerate((h0, h1, h2, h3)):
        h[...] = dot(low, weight[:, k * width : (k + 1) * width]).astype(BF16)
    sums[0:1, :] = jnp.sum(total, axis=0, keepdims=True)
    sums[1:2, :] = jnp.sum(grad * scaled, axis=0, keepdims=True)
    sums[2:3, :] = jnp.sum(grad, axis=0, keepdims=True)
    sums[3:4, :] = jnp.sum(upstream, axis=0, keepdims=True)


def join_kernel(f, f_received, o, o_received, total):
    columns = f.shape[2]
    for i in range(f.shape[0]):
        total[i, :, :columns] = (f[i].astype(F32) + f_received[i].astype(F32)).astype(BF16)
        total[i, :, columns:] = (o[i].astype(F32) + o_received[i].astype(F32)).astype(BF16)


def rows_back_kernel(p0, p1, p2, p3, source, gain, middle_grad, out):
    grad = p0[...].astype(F32)
    for p in (p1, p2, p3):
        grad = grad + p[...].astype(F32)
    scaled, inverse = scaled_rows(source[...].astype(F32))
    weighted = grad * gain[...]
    back = inverse * (
        weighted
        - jnp.mean(weighted, axis=-1, keepdims=True)
        - scaled * jnp.mean(weighted * scaled, axis=-1, keepdims=True)
    )
    out[...] = (middle_grad[...] + back).astype(BF16)


def shards(
    frames,
    attend_gain,
    attend_shift,
    query_weight,
    query_bias,
    key_weight,
    value_weight,
    value_bias,
    out_weight,
    out_bias,
    feed_gain,
    feed_shift,
    inner_weight,
    inner_bias,
    outer_weight,
    outer_bias,
    cotangent,
):
    position = lax.axis_index("mp")
    core = lax.axis_index("core")
    rows = frames.shape[1]
    length = rows * MP
    model = frames.shape[2]
    width = query_weight.shape[1]
    hidden = inner_weight.shape[1]
    depth = query_weight.shape[0]
    each = attend_gain.shape[0]
    heads = width // HD
    factor = HD ** (-0.5)
    slots = range(MP)
    core_index = core.reshape(1)
    position_index = position.reshape(1)

    vectors = 8 + MP
    pieces = (
        attend_gain,
        attend_shift,
        query_bias,
        value_bias,
        out_bias,
        feed_gain,
        feed_shift,
        outer_bias,
        inner_bias,
    )
    packed = sum(
        jnp.pad(v.astype(F32), (i * each, (8 + MP) * each - i * each - v.shape[0]))
        for i, v in enumerate(pieces)
    )
    entry = np.arange(vectors * each)
    early = entry < 8 * each
    row_of = np.where(early, entry % each, (entry - 8 * each) // MP)
    column_of = np.where(early, entry // each, 8 + (entry - 8 * each) % MP)
    to_column = jnp.asarray(column_of[:, None] == np.arange(vectors)[None], BF16)
    at_row = lax.iota(jnp.int32, depth)[:, None] == position * each + jnp.asarray(row_of, jnp.int32)
    piece = dot(jnp.where(at_row, packed[None], 0).astype(BF16), to_column).astype(BF16)
    carried = jnp.concatenate([turn_over(out_weight).astype(BF16), piece], axis=1)
    carried = [carried] + [shift_mp(carried, MP - k) for k in range(1, MP)]
    full_raw = lax.all_gather(frames[0], "mp", axis=0, tiled=True)
    (first_blocks,) = vmem_call(
        first_pack_kernel,
        [array((PLANE, depth, model + 3 * width + vectors))],
        10**6,
        *carried,
        query_weight,
        key_weight,
        value_weight,
        limit=52,
    )
    found = exchange_plane(first_blocks)
    inner_weight, outer_weight, found = lax.optimization_barrier(
        (inner_weight, outer_weight, found)
    )
    (feed_block,) = vmem_call(
        feed_pack_kernel, [array((depth, 2 * hidden))], 10**6, inner_weight, outer_weight.T, limit=4
    )
    feed_all = lax.all_gather(feed_block, ("yz", "core"), axis=0, tiled=True)
    first_all = join_cores(found, swap_cores(found), core)
    small = first_all[:, model + 3 * width :].T.astype(F32)
    first_norms = small[0:2]
    second_norms = jnp.stack([small[5], small[6], small[4]])
    local = lax.dynamic_slice_in_dim(small, position * width, width, axis=1)
    offset = jnp.concatenate([local[2], jnp.zeros_like(local[2]), local[3]])[None]
    inner_offset = local[8:].T.reshape(1, MP * width)

    rows_out = array((rows, model))
    heads_out = array((rows, width))
    normed, triple, turned_low, m0, m1, m2, m3, log_totals, kept = vmem_call(
        partial(attend_kernel, factor),
        [
            array((length, model)),
            array((length, 3 * width)),
            array((3 * width, length)),
            heads_out,
            heads_out,
            heads_out,
            heads_out,
            array((heads, length), F32),
            array((width, length), F32),
        ],
        4 * 10**9,
        position_index,
        full_raw,
        first_all,
        first_norms,
        offset,
        limit=18,
    )
    upstream_low = cotangent[0]
    ups = spread_rows(upstream_low)
    m1, m2, m3, *ups = lax.optimization_barrier((m1, m2, m3, *ups))
    own_mixed = [m0] + [shift_mp(m, MP - k) for k, m in ((1, m1), (2, m2), (3, m3))]
    own_mixed = list(lax.optimization_barrier(tuple(own_mixed)))
    middle, normed_two = vmem_call(
        middle_kernel,
        [array((rows, model), F32), rows_out],
        10**9,
        *own_mixed,
        first_all,
        frames[0],
        second_norms,
        limit=10,
    )
    twos = [normed_two, shift_mp(normed_two, 1), None, shift_mp(normed_two, MP - 1)]
    seconds, carry = {}, ()
    inner_sums = array((1, hidden), F32)
    feed_blocks = array((PLANE, depth, 2 * hidden))
    for k in (0, 1, 3, 2):
        last = k == 2
        grads = array((model, 2 * hidden), F32)
        fed_out = array((length, model))
        outs = [rows_out, feed_blocks, feed_blocks, fed_out, inner_sums]
        found = vmem_call(
            partial(feed_kernel, k, last),
            outs if last else [rows_out, grads, fed_out, inner_sums],
            5 * 10**9,
            position_index,
            core_index,
            twos[k],
            ups[k],
            feed_all,
            inner_offset,
            *carry,
            scratch=[pltpu.VMEM(grads.shape, F32)] if last else [],
            limit=16,
        )
        seconds[k] = found[0]
        if last:
            feed_mine, feed_other, fed_all, inner_total = found[1:]
        else:
            carry = found[1:]
        if k == 0:
            twos[1], twos[3], _ = lax.optimization_barrier((twos[1], twos[3], carry[2]))
            far = (shift_mp(twos[1][: rows // 2], 1), shift_mp(twos[3][rows // 2 :], MP - 1))
        if k == 3:
            *far, _ = lax.optimization_barrier((*far, carry[2]))
            twos[2] = jnp.concatenate(far)
    seconds = [seconds[0]] + [shift_mp(seconds[k], MP - k) for k in range(1, MP)]
    feed_mine, feed_other, seconds[1], seconds[3] = lax.optimization_barrier(
        (feed_mine, feed_other, seconds[1], seconds[3])
    )
    feed_total = feed_mine.astype(F32) + swap_cores(feed_other).astype(F32)
    feed_total = feed_total.astype(BF16)
    feed_total, seconds[2] = lax.optimization_barrier((feed_total, seconds[2]))
    feed_total = exchange_plane(feed_total)
    out_blocks = array((PLANE, depth, model))
    middle_grad, h0, h1, h2, h3, out_mine, out_other, middle_sums = vmem_call(
        middle_back_kernel,
        [
            array((rows, model), F32),
            *[heads_out] * MP,
            out_blocks,
            out_blocks,
            array((4, model), F32),
        ],
        10**9,
        core_index,
        *seconds,
        middle,
        upstream_low,
        second_norms,
        first_all,
        *own_mixed,
        scratch=[pltpu.VMEM((model, model), F32)],
        limit=52,
    )
    mixed_grads = [h0] + [shift_mp(h, k) for k, h in ((1, h1), (2, h2), (3, h3))]
    fed_all, *mixed_grads = lax.optimization_barrier((fed_all, *mixed_grads))
    fed = lax.psum_scatter(fed_all, "mp", scatter_dimension=0, tiled=True)
    out_other, h1 = lax.optimization_barrier((out_other, h1))
    out_received = swap_cores(out_other)
    blocks = array((PLANE, depth, 3 * width + vectors))
    *parts, last_mine, last_other = vmem_call(
        partial(attend_back_kernel, factor),
        [rows_out] * MP + [blocks, blocks],
        8 * 10**9,
        core_index,
        position_index,
        triple,
        turned_low,
        log_totals,
        kept,
        *mixed_grads,
        first_all,
        normed,
        first_norms,
        middle_sums,
        inner_total.reshape(width, MP),
        scratch=[
            pltpu.VMEM((length, 3 * width), F32),
            pltpu.VMEM((model, 3 * width + vectors), F32),
        ],
        limit=52,
    )
    last_mine, last_other, feed_total, out_received = lax.optimization_barrier(
        (last_mine, last_other, feed_total, out_received)
    )
    last_received = swap_cores(last_other)
    parts = [parts[0]] + [shift_mp(parts[k], MP - k) for k in range(1, MP)]
    (last_total,) = vmem_call(
        join_kernel,
        [array((PLANE, depth, 3 * width + vectors + model))],
        10**6,
        out_mine,
        out_received,
        last_mine,
        last_received,
        limit=14,
    )
    last_total = exchange_plane(last_total)
    last_total, fed, *parts = lax.optimization_barrier((last_total, fed, *parts))
    output = middle + small[7] + fed.astype(F32)
    output = output.astype(BF16)[None]
    feed_sums = jnp.sum(feed_total.astype(F32), axis=0)
    last_sums = jnp.sum(last_total.astype(F32), axis=0)
    tails = [
        jnp.concatenate(
            [
                last_sums[:, model + 3 * width :],
                last_sums[:, k * width : (k + 1) * width],
            ],
            axis=1,
        )
        for k in slots
    ]
    tail = tails[0] + sum(shift_mp(tails[k], k) for k in range(1, MP))
    pieces = lax.dynamic_slice_in_dim(tail, position * each, each, axis=0)
    inner_piece = pieces[:, 8:vectors].reshape(MP * each)
    (frames_grad,) = vmem_call(
        rows_back_kernel,
        [rows_out],
        10**8,
        *parts,
        frames[0],
        first_norms[0:1],
        middle_grad,
        limit=8,
    )
    return (
        output,
        frames_grad[None],
        pieces[:, 0],
        pieces[:, 1],
        last_sums[:, model : model + width],
        pieces[:, 6],
        last_sums[:, model + width : model + 2 * width],
        last_sums[:, model + 2 * width : model + 3 * width],
        pieces[:, 7],
        tail[:, vectors:].T,
        pieces[:, 2],
        pieces[:, 3],
        pieces[:, 4],
        feed_sums[:, :hidden],
        inner_piece,
        feed_sums[:, hidden : 2 * hidden].T,
        pieces[:, 5],
    )


def solution(mesh):
    mesh = Mesh(mesh.devices.reshape(PLANE, CORES, MP), ("yz", "core", "mp"))
    rows = P(("yz", "core"), "mp", None)
    vector = P(("yz", "core", "mp"))
    wide = P(("yz", "core"), "mp")
    tall = P("mp", ("yz", "core"))
    in_specs = (
        rows, vector, vector, wide, vector, wide, wide, vector, tall, vector,
        vector, vector, wide, vector, tall, vector, rows,
    )
    out_specs = (
        rows, rows, vector, vector, wide, vector, wide, wide, vector, tall,
        vector, vector, vector, wide, vector, tall, vector,
    )
    return jax.shard_map(shards, mesh=mesh, in_specs=in_specs, out_specs=out_specs, check_vma=False)
```
